256 devices in a mesh: expert: 8 (over z), dp: 32 (over x, y, core).
Axes of the slice: x: 4, y: 4, z: 8, core: 2. Of those that a mesh axis runs over, the one named last changes fastest.
Arguments:
- tokens: bfloat16 [1024, 4096], P('dp'), may hold values from -6 to 6
- cotangent: bfloat16 [1024, 4096], P('dp'), may hold values from -6 to 6
- routes: int32 [1024, 8], replicated, may hold values from 0 to 31, as said below
- slots: int32 [1024, 8], replicated, may hold values from 0 to 15, as said below
- combine: bfloat16 [1024, 8], replicated, may hold values from 0.099609375 to 0.59765625
- gate_weight: bfloat16 [256, 192, 4096], P(('expert', 'dp')), may hold values from -0.09375 to 0.09375
- up_weight: bfloat16 [256, 192, 4096], P(('expert', 'dp')), may hold values from -0.09375 to 0.09375
- down_weight: bfloat16 [256, 192, 4096], P(('expert', 'dp')), may hold values from -0.15625 to 0.15625
Outputs:
- mixed: bfloat16 [1024, 4096], P('dp', 'expert')
- tokens_grad: bfloat16 [1024, 4096], P('dp', 'expert')
- gate_grad_weight: bfloat16 [256, 192, 4096], P(('expert', 'dp'))
- up_grad_weight: bfloat16 [256, 192, 4096], P(('expert', 'dp'))
- down_grad_weight: bfloat16 [256, 192, 4096], P(('expert', 'dp'))
The draws below stay inside these ranges and needn't reach their ends.
Inputs may be any that keep to these rules, and one draw needn't show every extreme that they name: `routes`: each token names 8 different experts. In each token block no expert is named by more than 16 tokens; one expert is named by exactly 16 tokens in every block. Within one token block, the slots of the routes to one expert are 0 to their count - 1, each once.
All inputs are finite; a program needn't handle non-finite values.
Results may differ from the reference program's by a relative error of at most 0.02.
Values may be sent and summed in bfloat16 or wider, within the bound.
No kernel may reach another device: no remote copies, remote signals or barrier semaphores. Data moves between devices by JAX's collectives and lax.ppermute only.
A program may use at most 128 MiB of HBM per device.

```python
import jax
import jax.numpy as jnp
from jax import lax

D = 4096
FF = 1536
TOP = 8
TOK_DP = 32
EXPERTS = 32
SPLIT = 8
FF_SLICE = 192
CAP = 16
TOKENS = 1024
N_DP = 32


def route_plan(key):
    hot_key, column_keys = jax.random.split(key)
    hottest = jax.random.randint(hot_key, (), 0, EXPERTS)
    mean_load = TOK_DP * TOP // EXPERTS
    half_count = EXPERTS // 2
    places = jnp.arange(TOK_DP * TOP, dtype=jnp.int32)

    def one_column(column_key):
        key_delta, key_order, key_token = jax.random.split(column_key, 3)
        delta = jax.random.randint(key_delta, (half_count,), -mean_load, mean_load + 1)
        delta = delta.at[0].set(mean_load)
        counts = jnp.concatenate([mean_load + delta, mean_load - delta]).astype(jnp.int32)
        order = jax.random.permutation(key_order, EXPERTS).astype(jnp.int32)
        order = (order - order[0] + hottest) % EXPERTS
        ends = jnp.cumsum(counts).astype(jnp.int32)
        starts = ends - counts
        position = jnp.sum((ends[None, :] <= places[:, None]).astype(jnp.int32), axis=1)
        expert_of = order[position]
        slot_of = places - starts[position]
        relabel = jax.random.permutation(key_token, TOK_DP).astype(jnp.int32)
        token_of = relabel[places % TOK_DP]
        route_of = places // TOK_DP
        chosen = jnp.zeros((TOK_DP, TOP), jnp.int32).at[token_of, route_of].set(expert_of)
        slotted = jnp.zeros((TOK_DP, TOP), jnp.int32).at[token_of, route_of].set(slot_of)
        return (chosen, slotted)
    chosen, slotted = jax.vmap(one_column)(jax.random.split(column_keys, N_DP))
    return (chosen.reshape(TOKENS, TOP), slotted.reshape(TOKENS, TOP))


def draw_routes(key, part):
    return route_plan(key)[0]


def draw_slots(key, part):
    return route_plan(key)[1]


def level_of(stream_key, shape, pieces, smallest, high):
    gain = 1.0
    for axis_at, blocks in pieces:
        steps = jax.random.uniform(jax.random.fold_in(jax.random.fold_in(stream_key, 6), axis_at), (blocks,), jnp.float32, smallest / len(pieces), high / len(pieces))
        gain = gain * jnp.repeat(jnp.exp(steps), shape[axis_at] // blocks).reshape((-1,) + (1,) * (len(shape) - 1 - axis_at))
    return gain


def noise(rng, dims, scale, bound, shards=(), kind=jnp.bfloat16):
    array = jax.random.normal(rng, dims, jnp.float32) * scale
    if len(shards) > 0:
        array = level_of(rng, dims, shards, -0.22, 0.18) * array
    return jnp.clip(array, min=-bound, max=bound).astype(kind)


def setup_inputs(seed: int = 0) -> dict:
    splits = jax.random.split(jax.random.key(seed), 9)
    tokens = noise(splits[0], (TOKENS, D), 1.0, 6.0, ((0, 32),))
    cotangent = noise(splits[1], (TOKENS, D), 1.0, 6.0, ((0, 32),))
    routes = draw_routes(jax.random.fold_in(splits[8], 71), 0)
    slots = draw_slots(jax.random.fold_in(splits[8], 71), 0)
    combine = jnp.clip(jax.random.uniform(splits[4], (TOKENS, TOP), jnp.float32, 0.099609375, 0.59765625), 0.099609375, 0.59765625).astype(jnp.bfloat16)
    gate_weight = noise(splits[5], (EXPERTS * SPLIT, FF_SLICE, D), D ** -0.5, 0.09375, ((0, 256),))
    up_weight = noise(splits[6], (EXPERTS * SPLIT, FF_SLICE, D), D ** -0.5, 0.09375, ((0, 256),))
    down_weight = noise(splits[7], (EXPERTS * SPLIT, FF_SLICE, D), FF ** -0.5, 0.15625, ((0, 256),))
    return dict(tokens=tokens, cotangent=cotangent, routes=routes, slots=slots, combine=combine, gate_weight=gate_weight, up_weight=up_weight, down_weight=down_weight)


def slot_table(routes, slots, combine, expert):
    tokens_all = routes.shape[0]
    token_ids = jnp.arange(tokens_all, dtype=jnp.int32)
    dump = N_DP * CAP
    places = jnp.where(routes == expert, (token_ids // TOK_DP)[:, None] * CAP + slots, dump).reshape(-1).astype(jnp.int32)
    owners = jnp.broadcast_to(token_ids[:, None], routes.shape).reshape(-1)
    table = jnp.full((dump + 1,), tokens_all, jnp.int32).at[places].set(owners)
    weights = jnp.zeros((dump + 1,), jnp.float32).at[places].set(combine.astype(jnp.float32).reshape(-1))
    return table[:dump], weights[:dump]


def reference(tokens, cotangent, routes, slots, combine, gate_weight, up_weight, down_weight):
    padded_in = jnp.concatenate([tokens, jnp.zeros((1, D), tokens.dtype)], axis=0)
    padded_cot = jnp.concatenate([cotangent, jnp.zeros((1, D), cotangent.dtype)], axis=0)
    gate_all = gate_weight.reshape(EXPERTS, SPLIT, FF_SLICE, D)
    up_all = up_weight.reshape(EXPERTS, SPLIT, FF_SLICE, D)
    down_all = down_weight.reshape(EXPERTS, SPLIT, FF_SLICE, D)
    highest = lax.Precision.HIGHEST
    contract_last = (((1,), (1,)), ((), ()))
    contract_first = (((0,), (0,)), ((), ()))

    def one_expert(carry, expert):
        mixed_acc, grad_acc = carry
        table, weights = slot_table(routes, slots, combine, expert)
        rows_in = padded_in[table]
        rows_cot = padded_cot[table]
        gate_blocks = gate_all[expert]
        up_blocks = up_all[expert]
        down_blocks = down_all[expert]
        gate_full = gate_blocks.reshape(FF, D)
        up_full = up_blocks.reshape(FF, D)
        down_full = down_blocks.reshape(FF, D)
        gate_pre = lax.dot_general(rows_in, gate_full, contract_last, preferred_element_type=jnp.float32)
        up_pre = lax.dot_general(rows_in, up_full, contract_last, preferred_element_type=jnp.float32)
        gate_act = jax.nn.silu(gate_pre)
        hidden = (gate_act * up_pre).astype(jnp.bfloat16)
        outs = jnp.einsum("rsf,sfd->srd", hidden.astype(jnp.float32).reshape(-1, SPLIT, FF_SLICE), down_blocks.astype(jnp.float32), precision=highest)
        terms = (weights[None, :, None] * outs).astype(jnp.bfloat16)
        terms = lax.optimization_barrier(terms).astype(jnp.float32)
        mixed_acc = mixed_acc.at[table].add(jnp.sum(terms, axis=0))
        route_grad = (weights[:, None] * rows_cot.astype(jnp.float32)).astype(jnp.bfloat16)
        hidden_grad = lax.dot_general(route_grad, down_full, contract_last, preferred_element_type=jnp.float32)
        gate_sigmoid = jax.nn.sigmoid(gate_pre)
        up_grad = (hidden_grad * gate_act).astype(jnp.bfloat16)
        gate_grad = (hidden_grad * up_pre * gate_sigmoid * (1.0 + gate_pre * (1.0 - gate_sigmoid))).astype(jnp.bfloat16)
        back = jnp.einsum("rsf,sfd->srd", gate_grad.astype(jnp.float32).reshape(-1, SPLIT, FF_SLICE), gate_blocks.astype(jnp.float32), precision=highest)
        back = back + jnp.einsum("rsf,sfd->srd", up_grad.astype(jnp.float32).reshape(-1, SPLIT, FF_SLICE), up_blocks.astype(jnp.float32), precision=highest)
        back = lax.optimization_barrier(back.astype(jnp.bfloat16)).astype(jnp.float32)
        grad_acc = grad_acc.at[table].add(jnp.sum(back, axis=0))
        gate_wgrad = lax.dot_general(gate_grad, rows_in, contract_first, preferred_element_type=jnp.float32).astype(jnp.bfloat16)
        up_wgrad = lax.dot_general(up_grad, rows_in, contract_first, preferred_element_type=jnp.float32).astype(jnp.bfloat16)
        down_wgrad = lax.dot_general(hidden, route_grad, contract_first, preferred_element_type=jnp.float32).astype(jnp.bfloat16)
        gate_wgrad = gate_wgrad.reshape(SPLIT, FF_SLICE, D)
        up_wgrad = up_wgrad.reshape(SPLIT, FF_SLICE, D)
        down_wgrad = down_wgrad.reshape(SPLIT, FF_SLICE, D)
        return (mixed_acc, grad_acc), (gate_wgrad, up_wgrad, down_wgrad)

    start_acc = (jnp.zeros((TOKENS + 1, D), jnp.float32), jnp.zeros((TOKENS + 1, D), jnp.float32))
    (mixed_acc, grad_acc), (gate_grads, up_grads, down_grads) = lax.scan(one_expert, start_acc, jnp.arange(EXPERTS, dtype=jnp.int32))
    mixed = mixed_acc[:TOKENS].astype(jnp.bfloat16)
    tokens_grad = grad_acc[:TOKENS].astype(jnp.bfloat16)
    return (mixed, tokens_grad, gate_grads.reshape(EXPERTS * SPLIT, FF_SLICE, D), up_grads.reshape(EXPERTS * SPLIT, FF_SLICE, D), down_grads.reshape(EXPERTS * SPLIT, FF_SLICE, D))
```

```python
import jax
import jax.numpy as jnp
from jax import lax
from jax.sharding import Mesh, PartitionSpec as P

F32 = jnp.float32
BF16 = jnp.bfloat16
LAST = (((1,), (1,)), ((), ()))
FIRST = (((0,), (0,)), ((), ()))


def move(value, axis, offset):
    size = lax.axis_size(axis)
    return lax.ppermute(value, axis, [(i, (i + offset) % size) for i in range(size)])


def add(*terms):
    total = terms[0].astype(F32)
    for term in terms[1:]:
        total = total + term.astype(F32)
    return total.astype(BF16)


def to_expert(rows, cap):
    pieces = [rows[:cap]]
    for j in range(1, rows.shape[0] // cap):
        pieces.append(move(rows[j * cap : (j + 1) * cap], "x", j))
    return jnp.concatenate(pieces, axis=0)


def to_home(rows, cap):
    pieces = [rows[:cap]]
    for j in range(1, rows.shape[0] // cap):
        pieces.append(move(rows[j * cap : (j + 1) * cap], "x", -j))
    return jnp.concatenate(pieces, axis=0)


def gather_y(own):
    half = own.shape[0] // 2
    below = move(own, "y", 1)
    above = move(own, "y", -1)
    far = jnp.concatenate([move(below[:half], "y", 1), move(above[half:], "y", -1)], axis=0)
    near = [own, below, above]
    near = jnp.concatenate(near + [move(part, "c", 1) for part in near], axis=0)
    return near, jnp.concatenate([far, move(far, "c", 1)], axis=0)


def reduce_y(near, far):
    count = far.shape[0] // 2
    half = count // 2
    far = add(far[:count], move(far[count:], "c", 1))
    near = add(near[: 3 * count], move(near[3 * count :], "c", 1))
    own, below, above = near[:count], near[count : 2 * count], near[2 * count :]
    up = move(far[:half], "y", 1)
    down = move(far[half:], "y", -1)
    above = jnp.concatenate([add(above[:half], up), above[half:]], axis=0)
    below = jnp.concatenate([below[:half], add(below[half:], down)], axis=0)
    return add(own, move(above, "y", 1), move(below, "y", -1))


def reduce_z(whole):
    size = lax.axis_size("z")
    z = lax.axis_index("z")
    width = whole.shape[1] // size
    parts = []
    for k in range(size):
        part = lax.dynamic_slice_in_dim(whole, ((z + k) % size) * width, width, axis=1)
        parts.append(move(part, "z", k) if k else part)
    return add(*parts)


def forward(rows, gate, up, down):
    gate_pre = lax.dot_general(rows, gate, LAST, preferred_element_type=F32)
    up_pre = lax.dot_general(rows, up, LAST, preferred_element_type=F32)
    hidden = (jax.nn.silu(gate_pre) * up_pre).astype(BF16)
    terms = jnp.dot(hidden, down, preferred_element_type=F32).astype(BF16)
    return gate_pre, up_pre, hidden, terms


def backward(grads, gate_pre, up_pre, gate, up, down):
    hidden_grad = lax.dot_general(grads, down, LAST, preferred_element_type=F32)
    sigma = jax.nn.sigmoid(gate_pre)
    up_grad = (hidden_grad * jax.nn.silu(gate_pre)).astype(BF16)
    gate_grad = (hidden_grad * up_pre * sigma * (1.0 + gate_pre * (1.0 - sigma))).astype(BF16)
    back = jnp.dot(gate_grad, gate, preferred_element_type=F32)
    back = (back + jnp.dot(up_grad, up, preferred_element_type=F32)).astype(BF16)
    return gate_grad, up_grad, back


def local(tokens, cotangent, routes, slots, combine, gate_weight, up_weight, down_weight):
    group = lax.axis_size("x")
    count, routes_each = tokens.shape[0], routes.shape[1]
    cap = 2 * count * routes_each // (group * lax.axis_size("z"))
    x, y, c = lax.axis_index("x"), lax.axis_index("y"), lax.axis_index("c")
    block = (x * lax.axis_size("y") + y) * lax.axis_size("c") + c
    gate, up, down = gate_weight[0], up_weight[0], down_weight[0]

    def mine(table):
        return lax.dynamic_slice_in_dim(table, block * count, count, axis=0)

    place = lax.broadcasted_iota(jnp.int32, (group * cap, 1, 1), 0)
    expert = lax.axis_index("z") * group + (x + place // cap) % group
    hit = (mine(routes)[None] == expert) & (mine(slots)[None] == place % cap)
    picks = jnp.sum(hit.astype(F32), axis=2).astype(BF16)
    weights = jnp.sum(jnp.where(hit, mine(combine)[None].astype(F32), 0.0), axis=2).astype(BF16)

    sent_rows = jnp.dot(picks, tokens, preferred_element_type=F32).astype(BF16)
    sent_grads = jnp.dot(weights, cotangent, preferred_element_type=F32).astype(BF16)
    rows_near, rows_far = gather_y(to_expert(sent_rows, cap))
    grads_near, grads_far = gather_y(to_expert(sent_grads, cap))

    gate_near, up_near, hidden_near, terms_near = forward(rows_near, gate, up, down)
    gate_far, up_far, hidden_far, terms_far = forward(rows_far, gate, up, down)
    mixed = to_home(reduce_y(terms_near, terms_far), cap)
    mixed = lax.dot_general(weights, mixed, FIRST, preferred_element_type=F32).astype(BF16)
    mixed = reduce_z(mixed)

    ggrad_near, ugrad_near, back_near = backward(grads_near, gate_near, up_near, gate, up, down)
    ggrad_far, ugrad_far, back_far = backward(grads_far, gate_far, up_far, gate, up, down)
    tokens_grad = to_home(reduce_y(back_near, back_far), cap)
    tokens_grad = lax.dot_general(picks, tokens_grad, FIRST, preferred_element_type=F32)
    tokens_grad = reduce_z(tokens_grad.astype(BF16))

    rows = jnp.concatenate([rows_near, rows_far], axis=0)
    grads = jnp.concatenate([grads_near, grads_far], axis=0)

    def weight_grad(near, far, right):
        left = jnp.concatenate([near, far], axis=0)
        return lax.dot_general(left, right, FIRST, preferred_element_type=F32).astype(BF16)[None]

    return (
        mixed,
        tokens_grad,
        weight_grad(ggrad_near, ggrad_far, rows),
        weight_grad(ugrad_near, ugrad_far, rows),
        weight_grad(hidden_near, hidden_far, grads),
    )


def solution(mesh):
    shape = mesh.devices.shape
    fine = Mesh(mesh.devices.reshape(shape[0], 4, -1, 2), ("z", "x", "y", "c"))
    blocks = P(("x", "y", "c"), None)
    units = P(("z", "x", "y", "c"), None, None)
    return jax.shard_map(
        local,
        mesh=fine,
        in_specs=(blocks, blocks, P(), P(), P(), units, units, units),
        out_specs=(P(("x", "y", "c"), "z"), P(("x", "y", "c"), "z"), units, units, units),
        check_vma=False,
    )
```

```python
import jax
import jax.numpy as jnp
from jax import lax
from jax.sharding import Mesh, PartitionSpec as P

F32 = jnp.float32
BF16 = jnp.bfloat16
LAST = (((1,), (1,)), ((), ()))
FIRST = (((0,), (0,)), ((), ()))


def move(value, axis, offset):
    size = lax.axis_size(axis)
    return lax.ppermute(value, axis, [(i, (i + offset) % size) for i in range(size)])


def add(*terms):
    total = terms[0].astype(F32)
    for term in terms[1:]:
        total = total + term.astype(F32)
    return total.astype(BF16)


def to_expert(rows, cap):
    pieces = [rows[:cap]]
    for j in range(1, rows.shape[0] // cap):
        pieces.append(move(rows[j * cap : (j + 1) * cap], "x", j))
    return jnp.concatenate(pieces, axis=0)


def to_home(rows, cap):
    pieces = [rows[:cap]]
    for j in range(1, rows.shape[0] // cap):
        pieces.append(move(rows[j * cap : (j + 1) * cap], "x", -j))
    return jnp.concatenate(pieces, axis=0)


def gather_y(own):
    half = own.shape[0] // 2
    below = move(own, "y", 1)
    above = move(own, "y", -1)
    far = jnp.concatenate([move(below[:half], "y", 1), move(above[half:], "y", -1)], axis=0)
    near = [own, below, above]
    near = jnp.concatenate(near + [move(part, "c", 1) for part in near], axis=0)
    return near, jnp.concatenate([far, move(far, "c", 1)], axis=0)


def reduce_y(near, far):
    count = far.shape[0] // 2
    half = count // 2
    far = add(far[:count], move(far[count:], "c", 1))
    near = add(near[: 3 * count], move(near[3 * count :], "c", 1))
    own, below, above = near[:count], near[count : 2 * count], near[2 * count :]
    up = move(far[:half], "y", 1)
    down = move(far[half:], "y", -1)
    above = jnp.concatenate([add(above[:half], up), above[half:]], axis=0)
    below = jnp.concatenate([below[:half], add(below[half:], down)], axis=0)
    return add(own, move(above, "y", 1), move(below, "y", -1)), up


def exchange(value, axes):
    return lax.all_to_all(value, axes, 0, 0, tiled=True)


def forward(rows, gate, up, down):
    gate_pre = lax.dot_general(rows, gate, LAST, preferred_element_type=F32)
    up_pre = lax.dot_general(rows, up, LAST, preferred_element_type=F32)
    hidden = (jax.nn.silu(gate_pre) * up_pre).astype(BF16)
    terms = jnp.dot(hidden, down, preferred_element_type=F32).astype(BF16)
    return gate_pre, up_pre, hidden, terms


def backward(grads, gate_pre, up_pre, gate, up, down):
    hidden_grad = lax.dot_general(grads, down, LAST, preferred_element_type=F32)
    sigma = jax.nn.sigmoid(gate_pre)
    up_grad = (hidden_grad * jax.nn.silu(gate_pre)).astype(BF16)
    gate_grad = (hidden_grad * up_pre * sigma * (1.0 + gate_pre * (1.0 - sigma))).astype(BF16)
    back = jnp.dot(gate_grad, gate, preferred_element_type=F32)
    back = (back + jnp.dot(up_grad, up, preferred_element_type=F32)).astype(BF16)
    return gate_grad, up_grad, back


def local(tokens, cotangent, routes, slots, combine, gate_weight, up_weight, down_weight):
    group = lax.axis_size("x")
    count, routes_each = tokens.shape[0], routes.shape[1]
    cap = 2 * count * routes_each // (group * lax.axis_size("z"))
    x, y, c = lax.axis_index("x"), lax.axis_index("y"), lax.axis_index("c")
    block = (x * lax.axis_size("y") + y) * lax.axis_size("c") + c
    gate, up, down = gate_weight[0], up_weight[0], down_weight[0]

    def mine(table):
        return lax.dynamic_slice_in_dim(table, block * count, count, axis=0)

    place = lax.broadcasted_iota(jnp.int32, (group * cap, 1, 1), 0)
    expert = lax.axis_index("z") * group + (x + place // cap) % group
    hit = (mine(routes)[None] == expert) & (mine(slots)[None] == place % cap)
    picks = jnp.sum(hit.astype(F32), axis=2).astype(BF16)
    weights = jnp.sum(jnp.where(hit, mine(combine)[None].astype(F32), 0.0), axis=2).astype(BF16)

    sent_rows = jnp.dot(picks, tokens, preferred_element_type=F32).astype(BF16)
    sent_grads = jnp.dot(weights, cotangent, preferred_element_type=F32).astype(BF16)
    rows_near, rows_far = gather_y(to_expert(sent_rows, cap))
    grads_near, grads_far = gather_y(to_expert(sent_grads, cap))

    gate_near, up_near, hidden_near, terms_near = forward(rows_near, gate, up, down)
    gate_far, up_far, hidden_far, terms_far = forward(rows_far, gate, up, down)
    mixed, _ = reduce_y(terms_near, terms_far)
    mixed = to_home(mixed, cap)
    mixed = lax.dot_general(weights, mixed, FIRST, preferred_element_type=F32).astype(BF16)

    ggrad_near, ugrad_near, back_near = backward(grads_near, gate_near, up_near, gate, up, down)
    ggrad_far, ugrad_far, back_far = backward(grads_far, gate_far, up_far, gate, up, down)
    tokens_grad, passed = reduce_y(back_near, back_far)
    tokens_grad = to_home(tokens_grad, cap)
    tokens_grad = lax.dot_general(picks, tokens_grad, FIRST, preferred_element_type=F32)
    tokens_grad = tokens_grad.astype(BF16)

    hidden_far, ggrad_far, ugrad_far, _ = lax.optimization_barrier(
        (hidden_far, ggrad_far, ugrad_far, passed)
    )
    rows = jnp.concatenate([rows_near, rows_far], axis=0)
    grads = jnp.concatenate([grads_near, grads_far], axis=0)

    def weight_grad(near, far, right):
        left = jnp.concatenate([near, far], axis=0)
        return lax.dot_general(left, right, FIRST, preferred_element_type=F32).astype(BF16)[None]

    wgrads = (
        weight_grad(ggrad_near, ggrad_far, rows),
        weight_grad(ugrad_near, ugrad_far, rows),
        weight_grad(hidden_near, hidden_far, grads),
    )
    planes, width = lax.axis_size("z"), tokens.shape[1]
    both = jnp.concatenate([mixed, tokens_grad], axis=0).reshape(2 * count, planes, width // planes)
    both, wgrads = lax.optimization_barrier((both.transpose(1, 0, 2), wgrads))
    both = add(*exchange(both, "z"))
    return (both[:count], both[count:], *wgrads)


def solution(mesh):
    shape = mesh.devices.shape
    fine = Mesh(mesh.devices.reshape(shape[0], 4, -1, 2), ("z", "x", "y", "c"))
    blocks = P(("x", "y", "c"), None)
    units = P(("z", "x", "y", "c"), None, None)
    return jax.shard_map(
        local,
        mesh=fine,
        in_specs=(blocks, blocks, P(), P(), P(), units, units, units),
        out_specs=(P(("x", "y", "c"), "z"), P(("x", "y", "c"), "z"), units, units, units),
        check_vma=False,
    )
```

```python
import jax
import jax.numpy as jnp
from jax import lax
from jax.sharding import Mesh, PartitionSpec as P

F32 = jnp.float32
BF16 = jnp.bfloat16
LAST = (((1,), (1,)), ((), ()))
FIRST = (((0,), (0,)), ((), ()))


def move(value, axis, offset):
    size = lax.axis_size(axis)
    return lax.ppermute(value, axis, [(i, (i + offset) % size) for i in range(size)])


def add(*terms):
    total = terms[0].astype(F32)
    for term in terms[1:]:
        total = total + term.astype(F32)
    return total.astype(BF16)


def to_expert(rows, cap):
    pieces = [rows[:cap]]
    for j in range(1, rows.shape[0] // cap):
        pieces.append(move(rows[j * cap : (j + 1) * cap], "x", j))
    return jnp.concatenate(pieces, axis=0)


def to_home(rows, cap):
    pieces = [rows[:cap]]
    for j in range(1, rows.shape[0] // cap):
        pieces.append(move(rows[j * cap : (j + 1) * cap], "x", -j))
    return jnp.concatenate(pieces, axis=0)


def gather_y(own):
    half = own.shape[0] // 2
    below = move(own, "y", 1)
    above = move(own, "y", -1)
    far = jnp.concatenate([move(below[:half], "y", 1), move(above[half:], "y", -1)], axis=0)
    near = [own, below, above]
    near = jnp.concatenate(near, axis=0)
    near = jnp.concatenate([near, move(near, "c", 1)], axis=0)
    return near, jnp.concatenate([far, move(far, "c", 1)], axis=0)


def reduce_y(near, far):
    count = far.shape[0] // 2
    half = count // 2
    far = add(far[:count], move(far[count:], "c", 1))
    near = add(near[: 3 * count], move(near[3 * count :], "c", 1))
    own, below, above = near[:count], near[count : 2 * count], near[2 * count :]
    up = move(far[:half], "y", 1)
    down = move(far[half:], "y", -1)
    above = jnp.concatenate([add(above[:half], up), above[half:]], axis=0)
    below = jnp.concatenate([below[:half], add(below[half:], down)], axis=0)
    return own, move(above, "y", 1), move(below, "y", -1)


def exchange(value, axes):
    return lax.all_to_all(value, axes, 0, 0, tiled=True)


def forward(rows, gate, up, down):
    gate_pre = lax.dot_general(rows, gate, LAST, preferred_element_type=F32)
    up_pre = lax.dot_general(rows, up, LAST, preferred_element_type=F32)
    hidden = (jax.nn.silu(gate_pre) * up_pre).astype(BF16)
    terms = jnp.dot(hidden, down, preferred_element_type=F32).astype(BF16)
    return gate_pre, up_pre, hidden, terms


def backward(grads, gate_pre, up_pre, gate, up, down):
    hidden_grad = lax.dot_general(grads, down, LAST, preferred_element_type=F32)
    sigma = jax.nn.sigmoid(gate_pre)
    up_grad = (hidden_grad * jax.nn.silu(gate_pre)).astype(BF16)
    gate_grad = (hidden_grad * up_pre * sigma * (1.0 + gate_pre * (1.0 - sigma))).astype(BF16)
    back = jnp.dot(gate_grad, gate, preferred_element_type=F32)
    back = (back + jnp.dot(up_grad, up, preferred_element_type=F32)).astype(BF16)
    return gate_grad, up_grad, back


def local(tokens, cotangent, routes, slots, combine, gate_weight, up_weight, down_weight):
    group = lax.axis_size("x")
    count, routes_each = tokens.shape[0], routes.shape[1]
    cap = 2 * count * routes_each // (group * lax.axis_size("z"))
    x, y, c = lax.axis_index("x"), lax.axis_index("y"), lax.axis_index("c")
    block = (x * lax.axis_size("y") + y) * lax.axis_size("c") + c
    gate, up, down = gate_weight[0], up_weight[0], down_weight[0]

    def mine(table):
        return lax.dynamic_slice_in_dim(table, block * count, count, axis=0)

    place = lax.broadcasted_iota(jnp.int32, (group * cap, 1, 1), 0)
    expert = lax.axis_index("z") * group + (x + place // cap) % group
    hit = (mine(routes)[None] == expert) & (mine(slots)[None] == place % cap)
    picks = jnp.sum(hit.astype(F32), axis=2).astype(BF16)
    weights = jnp.sum(jnp.where(hit, mine(combine)[None].astype(F32), 0.0), axis=2).astype(BF16)

    sent_rows = jnp.dot(picks, tokens, preferred_element_type=F32).astype(BF16)
    sent_grads = jnp.dot(weights, cotangent, preferred_element_type=F32).astype(BF16)
    rows_near, rows_far = gather_y(to_expert(sent_rows, cap))
    grads_near, grads_far = gather_y(to_expert(sent_grads, cap))

    gate_near, up_near, hidden_near, terms_near = forward(rows_near, gate, up, down)
    gate_far, up_far, hidden_far, terms_far = forward(rows_far, gate, up, down)
    summed = add(*reduce_y(terms_near, terms_far))
    mixed = to_home(summed, cap)
    mixed = lax.dot_general(weights, mixed, FIRST, preferred_element_type=F32).astype(BF16)

    ggrad_near, ugrad_near, back_near = backward(grads_near, gate_near, up_near, gate, up, down)
    ggrad_far, ugrad_far, back_far = backward(grads_far, gate_far, up_far, gate, up, down)
    sums = reduce_y(back_near, back_far)
    hidden_far, ggrad_far, ugrad_far, _ = lax.optimization_barrier(
        (hidden_far, ggrad_far, ugrad_far, summed)
    )
    rows = jnp.concatenate([rows_near, rows_far], axis=0)
    grads = jnp.concatenate([grads_near, grads_far], axis=0)

    def weight_grad(near, far, right):
        left = jnp.concatenate([near, far], axis=0)
        return lax.dot_general(left, right, FIRST, preferred_element_type=F32).astype(BF16)[None]

    wgrads = (
        weight_grad(ggrad_near, ggrad_far, rows),
        weight_grad(ugrad_near, ugrad_far, rows),
        weight_grad(hidden_near, hidden_far, grads),
    )
    sums, wgrads = lax.optimization_barrier((sums, wgrads))
    tokens_grad = add(*sums)
    tokens_grad = to_home(tokens_grad, cap)
    tokens_grad = lax.dot_general(picks, tokens_grad, FIRST, preferred_element_type=F32)
    tokens_grad = tokens_grad.astype(BF16)

    planes, width = lax.axis_size("z"), tokens.shape[1]
    both = jnp.concatenate([mixed, tokens_grad], axis=0).reshape(2 * count, planes, width // planes)
    both, wgrads = lax.optimization_barrier((both.transpose(1, 0, 2), wgrads))
    both = add(*exchange(both, "z"))
    return (both[:count], both[count:], *wgrads)


def solution(mesh):
    shape = mesh.devices.shape
    fine = Mesh(mesh.devices.reshape(shape[0], 4, -1, 2), ("z", "x", "y", "c"))
    blocks = P(("x", "y", "c"), None)
    units = P(("z", "x", "y", "c"), None, None)
    return jax.shard_map(
        local,
        mesh=fine,
        in_specs=(blocks, blocks, P(), P(), P(), units, units, units),
        out_specs=(P(("x", "y", "c"), "z"), P(("x", "y", "c"), "z"), units, units, units),
        check_vma=False,
    )
```

```python
import jax
import jax.numpy as jnp
from jax import lax
from jax.sharding import Mesh, PartitionSpec as P

F32 = jnp.float32
BF16 = jnp.bfloat16
LAST = (((1,), (1,)), ((), ()))
FIRST = (((0,), (0,)), ((), ()))


def move(value, axis, offset):
    size = lax.axis_size(axis)
    return lax.ppermute(value, axis, [(i, (i + offset) % size) for i in range(size)])


def add(*terms):
    total = terms[0].astype(F32)
    for term in terms[1:]:
        total = total + term.astype(F32)
    return total.astype(BF16)


def to_expert(rows, cap):
    pieces = [rows[:cap]]
    for j in range(1, rows.shape[0] // cap):
        pieces.append(move(rows[j * cap : (j + 1) * cap], "x", j))
    return jnp.concatenate(pieces, axis=0)


def to_home(rows, cap):
    pieces = [rows[:cap]]
    for j in range(1, rows.shape[0] // cap):
        pieces.append(move(rows[j * cap : (j + 1) * cap], "x", -j))
    return jnp.concatenate(pieces, axis=0)


def gather_y(own):
    half = own.shape[0] // 2
    below = move(own, "y", 1)
    above = move(own, "y", -1)
    far = jnp.concatenate([move(below[:half], "y", 1), move(above[half:], "y", -1)], axis=0)
    near = [own, below, above]
    near = jnp.concatenate(near, axis=0)
    near = jnp.concatenate([near, move(near, "c", 1)], axis=0)
    return near, jnp.concatenate([far, move(far, "c", 1)], axis=0)


def reduce_y(near, far):
    count = far.shape[0] // 2
    half = count // 2
    far = add(far[:count], move(far[count:], "c", 1))
    near = add(near[: 3 * count], move(near[3 * count :], "c", 1))
    own, below, above = near[:count], near[count : 2 * count], near[2 * count :]
    up = move(far[:half], "y", 1)
    down = move(far[half:], "y", -1)
    above = jnp.concatenate([add(above[:half], up), above[half:]], axis=0)
    below = jnp.concatenate([below[:half], add(below[half:], down)], axis=0)
    return own, move(above, "y", 1), move(below, "y", -1)


def exchange(value, axes):
    return lax.all_to_all(value, axes, 0, 0, tiled=True)


def forward(rows, gate, up, down):
    gate_pre = lax.dot_general(rows, gate, LAST, preferred_element_type=F32)
    up_pre = lax.dot_general(rows, up, LAST, preferred_element_type=F32)
    hidden = (jax.nn.silu(gate_pre) * up_pre).astype(BF16)
    terms = jnp.dot(hidden, down, preferred_element_type=F32).astype(BF16)
    return gate_pre, up_pre, hidden, terms


def backward(grads, gate_pre, up_pre, gate_up, down):
    hidden_grad = lax.dot_general(grads, down, LAST, preferred_element_type=F32)
    sigma = jax.nn.sigmoid(gate_pre)
    up_grad = (hidden_grad * jax.nn.silu(gate_pre)).astype(BF16)
    gate_grad = (hidden_grad * up_pre * sigma * (1.0 + gate_pre * (1.0 - sigma))).astype(BF16)
    both = jnp.concatenate([gate_grad, up_grad], axis=1)
    back = jnp.dot(both, gate_up, preferred_element_type=F32).astype(BF16)
    return gate_grad, up_grad, back


def local(tokens, cotangent, routes, slots, combine, gate_weight, up_weight, down_weight):
    group = lax.axis_size("x")
    count, routes_each = tokens.shape[0], routes.shape[1]
    cap = 2 * count * routes_each // (group * lax.axis_size("z"))
    x, y, c = lax.axis_index("x"), lax.axis_index("y"), lax.axis_index("c")
    block = (x * lax.axis_size("y") + y) * lax.axis_size("c") + c
    gate, up, down = gate_weight[0], up_weight[0], down_weight[0]
    gate_up = lax.optimization_barrier(jnp.concatenate([gate, up], axis=0))

    def mine(table):
        return lax.dynamic_slice_in_dim(table, block * count, count, axis=0)

    place = lax.broadcasted_iota(jnp.int32, (group * cap, 1, 1), 0)
    expert = lax.axis_index("z") * group + (x + place // cap) % group
    hit = (mine(routes)[None] == expert) & (mine(slots)[None] == place % cap)
    picks = jnp.sum(hit.astype(F32), axis=2).astype(BF16)
    weights = jnp.sum(jnp.where(hit, mine(combine)[None].astype(F32), 0.0), axis=2).astype(BF16)

    sent_rows = jnp.dot(picks, tokens, preferred_element_type=F32).astype(BF16)
    sent_grads = jnp.dot(weights, cotangent, preferred_element_type=F32).astype(BF16)
    rows_near, rows_far = gather_y(to_expert(sent_rows, cap))
    grads_near, grads_far = gather_y(to_expert(sent_grads, cap))

    gate_near, up_near, hidden_near, terms_near = forward(rows_near, gate, up, down)
    gate_far, up_far, hidden_far, terms_far = forward(rows_far, gate, up, down)
    summed = add(*reduce_y(terms_near, terms_far))
    mixed = to_home(summed, cap)
    mixed = lax.dot_general(weights, mixed, FIRST, preferred_element_type=F32).astype(BF16)

    ggrad_near, ugrad_near, back_near = backward(grads_near, gate_near, up_near, gate_up, down)
    ggrad_far, ugrad_far, back_far = backward(grads_far, gate_far, up_far, gate_up, down)
    sums = reduce_y(back_near, back_far)
    hidden_far, ggrad_far, ugrad_far, _ = lax.optimization_barrier(
        (hidden_far, ggrad_far, ugrad_far, summed)
    )
    rows = jnp.concatenate([rows_near, rows_far], axis=0)
    grads = jnp.concatenate([grads_near, grads_far], axis=0)

    def weight_grad(near, far, right):
        left = jnp.concatenate([near, far], axis=0)
        return lax.dot_general(left, right, FIRST, preferred_element_type=F32).astype(BF16)[None]

    wgrads = (
        weight_grad(ggrad_near, ggrad_far, rows),
        weight_grad(ugrad_near, ugrad_far, rows),
        weight_grad(hidden_near, hidden_far, grads),
    )
    sums, wgrads = lax.optimization_barrier((sums, wgrads))
    tokens_grad = add(*sums)
    tokens_grad = to_home(tokens_grad, cap)
    tokens_grad = lax.dot_general(picks, tokens_grad, FIRST, preferred_element_type=F32)
    tokens_grad = tokens_grad.astype(BF16)

    planes, width = lax.axis_size("z"), tokens.shape[1]
    both = jnp.concatenate([mixed, tokens_grad], axis=0).reshape(2 * count, planes, width // planes)
    both, wgrads = lax.optimization_barrier((both.transpose(1, 0, 2), wgrads))
    both = add(*exchange(both, "z"))
    return (both[:count], both[count:], *wgrads)


def solution(mesh):
    shape = mesh.devices.shape
    fine = Mesh(mesh.devices.reshape(shape[0], 4, -1, 2), ("z", "x", "y", "c"))
    blocks = P(("x", "y", "c"), None)
    units = P(("z", "x", "y", "c"), None, None)
    return jax.shard_map(
        local,
        mesh=fine,
        in_specs=(blocks, blocks, P(), P(), P(), units, units, units),
        out_specs=(P(("x", "y", "c"), "z"), P(("x", "y", "c"), "z"), units, units, units),
        check_vma=False,
    )
```
